32 devices in a mesh: gx: 8 (over y, x, core), gy: 4 (over z).
Axes of the slice: x: 2, y: 2, z: 4, core: 2. Of those that a mesh axis runs over, the one named last changes fastest.
Arguments:
- fields: float32 [6, 128, 128, 128], P(None, 'gx', 'gy'), may hold values from -0.0029296875 to 0.0029296875
- region: int32 [128, 128, 128], P('gx', 'gy'), may hold values from 0 to 15
- eps_table: float32 [16], replicated, may hold values from 1 to 2
Outputs:
- advanced: float32 [6, 128, 128, 128], P(None, 'gx', 'gy')
The draws below stay inside these ranges and needn't reach their ends.
All inputs are finite; a program needn't handle non-finite values.
Results may differ from the reference program's by a relative error of at most 0.0003.
Values sent between devices are 32-bit elements; how exact they have to be, the bound alone decides.
A program may use at most 128 MiB of HBM per device.

```python
import math
import jax
import jax.numpy as jnp
from jax import lax

NZ = 128
REGIONS = 16
NX = 128
NY = 128


def set_ends(values, key, least, high):
    index_at = [jax.random.randint(jax.random.fold_in(key, axis), (), 0, length) for axis, length in enumerate(values.shape)]
    main_axis = values.shape.index(max(values.shape))
    neighbour = index_at[:main_axis] + [(index_at[main_axis] + 1) % values.shape[main_axis]] + index_at[main_axis + 1:]
    return values.at[tuple(index_at)].set(least).at[tuple(neighbour)].set(high)


def levels(stream_key, extent, pieces, low, top_value):
    def one(dim, blocks):
        steps = jax.random.uniform(jax.random.fold_in(jax.random.fold_in(stream_key, 6), dim), (blocks,), jnp.float32, low / len(pieces), top_value / len(pieces))
        return jnp.repeat(jnp.exp(steps), extent[dim] // blocks).reshape((-1,) + (1,) * (len(extent) - dim - 1))

    loudness = one(*pieces[0])
    for cut in pieces[1:]:
        loudness = loudness * one(*cut)
    return loudness


def scatter_about(key, extent, deviation, bound, cuts=(), dtype=jnp.bfloat16):
    level = levels(key, extent, cuts, -0.22, 0.18) if cuts else 1.0
    values = jax.random.normal(key, extent, jnp.float32) * deviation * level
    return jnp.minimum(jnp.maximum(values, -bound), bound).astype(dtype)


def setup_inputs(seed: int = 0) -> dict:
    keys = jax.random.split(jax.random.key(seed), 4)
    fields = scatter_about(keys[0], (6, NX, NY, NZ), 0.0005, 0.0029296875, ((1, 8), (2, 4)), jnp.float32)
    region = set_ends(jax.random.randint(keys[1], (NX, NY, NZ), 0, REGIONS), jax.random.fold_in(keys[1], 1), 0, REGIONS - 1).astype(jnp.int32)
    eps_table = jnp.clip(jnp.exp(jax.random.uniform(keys[2], (REGIONS,), jnp.float32, math.log(1.0), math.log(2.0))), 1.0, 2.0)
    return {"fields": fields, "region": region, "eps_table": eps_table}


plane_ratio = 32.0
depth_ratio = 0.5


def step_next(values, along_axis):
    tail_zeros = jnp.zeros_like(lax.slice_in_dim(values, 0, 1, axis=along_axis))
    shifted = jnp.concatenate([lax.slice_in_dim(values, 1, values.shape[along_axis], axis=along_axis), tail_zeros], axis=along_axis)
    return shifted - values


def step_prev(values, along_axis):
    head_zeros = jnp.zeros_like(lax.slice_in_dim(values, 0, 1, axis=along_axis))
    shifted = jnp.concatenate([head_zeros, lax.slice_in_dim(values, 0, values.shape[along_axis] - 1, axis=along_axis)], axis=along_axis)
    return values - shifted


def solve_lines(coupling, right_side):
    length = coupling.shape[0]
    position = jnp.arange(length)[:, None, None]
    lower_band = jnp.where(position > 0, -coupling, 0.0 * coupling)
    upper_band = jnp.where(position < length - 1, -coupling, 0.0 * coupling)
    diagonal = 1.0 + coupling * jnp.where(position == 0, 1.0, 2.0)

    def forward_step(carried, entries):
        carried_upper, carried_source = carried
        lower_row, diag_row, upper_row, source = entries
        divisor = diag_row - lower_row * carried_upper
        new_upper = upper_row / divisor
        new_source = (source - lower_row * carried_source) / divisor
        return (new_upper, new_source), (new_upper, new_source)

    start_row = jnp.zeros_like(coupling[0])
    _, (uppers, sources) = lax.scan(forward_step, (start_row, start_row), (lower_band, diagonal, upper_band, right_side))

    def backward_step(behind, entries):
        upper_row, source = entries
        solved = source - upper_row * behind
        return solved, solved

    _, solution = lax.scan(backward_step, start_row, (uppers, sources), reverse=True)
    return solution


def solve_x(coupling, right_side):
    return solve_lines(coupling, right_side)


def solve_y(coupling, right_side):
    solved = solve_lines(jnp.swapaxes(coupling, 0, 1), jnp.swapaxes(right_side, 0, 1))
    return jnp.swapaxes(solved, 0, 1)


def reference(fields, region, eps_table):
    inv_eps = (1.0 / eps_table)[region]
    plane_coef = plane_ratio * inv_eps
    depth_coef = depth_ratio * inv_eps
    coupling = plane_ratio * plane_coef
    ex_now = fields[0]
    ey_now = fields[1]
    ez_now = fields[2]
    hx_now = fields[3]
    hy_now = fields[4]
    hz_now = fields[5]
    partial_hz = hz_now - plane_ratio * step_next(ey_now, 0)
    partial_hy = hy_now - depth_ratio * step_next(ex_now, 2)
    ey_one = ey_now + depth_coef * step_prev(hx_now, 2) - plane_coef * step_prev(hz_now, 0)
    ex_one = solve_y(coupling, ex_now + plane_coef * step_prev(partial_hz, 1) - depth_coef * step_prev(hy_now, 2))
    ez_one = solve_x(coupling, ez_now + plane_coef * step_prev(partial_hy, 0) - plane_coef * step_prev(hx_now, 1))
    hz_one = partial_hz + plane_ratio * step_next(ex_one, 1)
    hy_one = partial_hy + plane_ratio * step_next(ez_one, 0)
    hx_one = hx_now - plane_ratio * step_next(ez_one, 1) + depth_ratio * step_next(ey_one, 2)
    ex_two = ex_one + plane_coef * step_prev(hz_one, 1) - depth_coef * step_prev(hy_one, 2)
    partial_z = hz_one + plane_ratio * step_next(ex_one, 1)
    partial_x = hx_one + depth_ratio * step_next(ey_one, 2)
    ey_two = solve_x(coupling, ey_one + depth_coef * step_prev(hx_one, 2) - plane_coef * step_prev(partial_z, 0))
    ez_two = solve_y(coupling, ez_one + plane_coef * step_prev(hy_one, 0) - plane_coef * step_prev(partial_x, 1))
    hz_two = partial_z - plane_ratio * step_next(ey_two, 0)
    hx_two = partial_x - plane_ratio * step_next(ez_two, 1)
    hy_two = hy_one - depth_ratio * step_next(ex_two, 2) + plane_ratio * step_next(ez_two, 0)
    return jnp.stack([ex_two, ey_two, ez_two, hx_two, hy_two, hz_two])
```

```python
import functools

import jax
import jax.numpy as jnp
from jax import lax
from jax.experimental import pallas as pl
from jax.experimental.pallas import tpu as pltpu
from jax.sharding import PartitionSpec as P

MESH = pl.DeviceIdType.MESH
EX, EY, EZ, HX, HY, HZ = range(6)


def kernel(
    n, m, nx, ny, nz, labels,
    fields, region, eps, out,
    ce, inv_x, c_x, l_x, r_x, inv_y, c_y, l_y, r_y,
    p_x, p_y, rhs, p1, ey1, ez1, ex1, p2,
    ey_next, hz_prev, hx_prev, hx_send, ez_next, ez_send, v_next, wr_x, wr_y,
    mx_send, mx_recv, gx_one, gx_two, coef_x, sx_send, sx_recv,
    my_send, my_recv, gy_one, gy_two, coef_y, sy_send, sy_recv,
    near_send, near_recv, x_send, x_recv, y_send, y_recv,
):
    gx = lax.axis_index("gx")
    gy = lax.axis_index("gy")

    barrier = pltpu.get_barrier_semaphore()
    for k in range(1, n):
        pl.semaphore_signal(
            barrier, inc=1, device_id={"gx": lax.rem(gx + k, n)}, device_id_type=MESH
        )
    for k in range(1, m):
        pl.semaphore_signal(
            barrier, inc=1, device_id={"gy": lax.rem(gy + k, m)}, device_id_type=MESH
        )

    def plane(i):
        return pl.ds(pl.multiple_of(i * ny, ny), ny)

    def row(j):
        return pl.ds(pl.multiple_of(j * nx, nx), nx)

    def across(j):
        return pl.ds(j, nx, stride=ny)

    lane = lax.broadcasted_iota(jnp.int32, (ny, nz), 1)
    sub = lax.broadcasted_iota(jnp.int32, (ny, nz), 0)
    zero_plane = jnp.zeros((ny, nz), jnp.float32)
    zero_row = jnp.zeros((nx, nz), jnp.float32)

    def f_z(v):
        return jnp.where(lane == nz - 1, 0.0, pltpu.roll(v, nz - 1, 1)) - v

    def b_z(v):
        return v - jnp.where(lane == 0, 0.0, pltpu.roll(v, 1, 1))

    def f_y(v, after):
        return jnp.where(sub == ny - 1, after, pltpu.roll(v, ny - 1, 0)) - v

    def b_y(v, before):
        return v - jnp.where(sub == 0, before, pltpu.roll(v, 1, 0))

    def near(src, dst, slot, device):
        return pltpu.make_async_remote_copy(
            src_ref=src, dst_ref=dst, send_sem=near_send.at[slot],
            recv_sem=near_recv.at[slot], device_id=device, device_id_type=MESH,
        )

    to_left = {"gx": jnp.maximum(gx - 1, 0)}
    to_right = {"gx": jnp.minimum(gx + 1, n - 1)}
    to_low = {"gy": jnp.maximum(gy - 1, 0)}
    to_high = {"gy": jnp.minimum(gy + 1, m - 1)}
    send_ey = near(fields.at[EY, pl.ds(0, ny)], ey_next, 0, to_left)
    send_hz = near(fields.at[HZ, pl.ds((nx - 1) * ny, ny)], hz_prev, 1, to_right)
    send_hx = near(hx_send, hx_prev, 2, to_high)
    send_ez = near(ez_send, ez_next, 3, to_low)
    send_v = near(rhs.at[pl.ds(0, ny)], v_next, 4, to_left)

    has_left = gx > 0
    has_right = gx < n - 1
    has_low = gy > 0
    has_high = gy < m - 1

    def start(cond, copy):
        @pl.when(cond)
        def _():
            copy.start()

    def sent(cond, copy):
        @pl.when(cond)
        def _():
            copy.wait_send()

    def arrived(cond, copy, ref):
        @pl.when(cond)
        def _():
            copy.wait_recv()

        @pl.when(jnp.logical_not(cond))
        def _():
            ref[...] = jnp.zeros(ref.shape, jnp.float32)

    hx_send[...] = fields[HX, across(ny - 1), :]

    def x_copy(kind, k, src, dst):
        target = lax.rem(gx + k, n)
        return pltpu.make_async_remote_copy(
            src_ref=src, dst_ref=dst.at[gx], send_sem=x_send.at[kind, k],
            recv_sem=x_recv.at[kind, gx], device_id={"gx": target}, device_id_type=MESH,
        )

    def y_copy(kind, k, src, dst):
        target = lax.rem(gy + k, m)
        return pltpu.make_async_remote_copy(
            src_ref=src, dst_ref=dst.at[gy], send_sem=y_send.at[kind, k],
            recv_sem=y_recv.at[kind, gy], device_id={"gy": target}, device_id_type=MESH,
        )

    def x_wait(kind, src, dst, j):
        pltpu.make_async_remote_copy(
            src_ref=src, dst_ref=dst.at[j], send_sem=x_send.at[kind, 0],
            recv_sem=x_recv.at[kind, j], device_id={"gx": j}, device_id_type=MESH,
        ).wait_recv()

    def y_wait(kind, src, dst, j):
        pltpu.make_async_remote_copy(
            src_ref=src, dst_ref=dst.at[j], send_sem=y_send.at[kind, 0],
            recv_sem=y_recv.at[kind, j], device_id={"gy": j}, device_id_type=MESH,
        ).wait_recv()

    pl.semaphore_wait(barrier, n + m - 2)
    start(has_left, send_ey)
    start(has_high, send_hx)
    start(has_right, send_hz)

    def pick(label, lowest, width):
        if width == 1:
            return eps[lowest]
        half = width // 2
        return jnp.where(
            (label & half) != 0,
            pick(label, lowest + half, half),
            pick(label, lowest, half),
        )

    def coefficients(i, _):
        s = plane(i)
        label = region[s, :]
        ce[s, :] = 32.0 / pick(label, 0, labels)
        return 0

    lax.fori_loop(0, nx, coefficients, 0)

    def factor(count, load_ce, at, first, zero, inv_ref, c_ref, l_ref, r_ref, send_ref):
        ones = zero + 1.0

        def forward(i, carry):
            c_last, d_last = carry
            kk = 32.0 * load_ce(i)
            inv = 1.0 / (1.0 + (2.0 * kk - kk * c_last))
            c = kk * inv
            d = c * d_last
            s = at(i)
            inv_ref[s, :] = inv
            c_ref[s, :] = c
            l_ref[s, :] = d
            return c, d

        lax.fori_loop(0, count, forward, (zero + jnp.where(first, 1.0, 0.0), ones))

        def backward(t, carry):
            l_after, r_after = carry
            s = at(count - 1 - t)
            c = c_ref[s, :]
            l = l_ref[s, :] + c * l_after
            r = c * r_after
            l_ref[s, :] = l
            r_ref[s, :] = r
            return l, r

        l_first, r_first = lax.fori_loop(0, count, backward, (zero, ones))
        send_ref[0] = l_first
        send_ref[1] = r_ref[at(count - 1), :]
        send_ref[2] = r_first

    factor(nx, lambda i: ce[plane(i), :], plane, gx == 0, zero_plane,
           inv_x, c_x, l_x, r_x, mx_send)
    for k in range(1, n):
        x_copy(0, k, mx_send, mx_recv).start()
    factor(ny, lambda j: ce[across(j), :], row, gy == 0, zero_row,
           inv_y, c_y, l_y, r_y, my_send)
    for k in range(1, m):
        y_copy(0, k, my_send, my_recv).start()

    def backward_sweep(count, at, zero, c_ref, p_ref):
        def body(t, after):
            s = at(count - 1 - t)
            w = p_ref[s, :] + c_ref[s, :] * after
            p_ref[s, :] = w
            return w

        return lax.fori_loop(0, count, body, zero)

    def y_sweep():
        def body(j, last):
            s = row(j)
            d = rhs[across(j), :] * inv_y[s, :] + c_y[s, :] * last
            p_y[s, :] = d
            return d

        last = lax.fori_loop(0, ny, body, zero_row)
        return backward_sweep(ny, row, zero_row, c_y, p_y), last

    arrived(has_low, send_hx, hx_prev)

    def ez_forward(i, carry):
        q_last, d_last = carry
        s = plane(i)
        q = fields[HY, s, :] - 0.5 * f_z(fields[EX, s, :])
        coef = ce[s, :]
        r = fields[EZ, s, :] + coef * (
            (q - q_last) - b_y(fields[HX, s, :], hx_prev[pl.ds(i, 1), :])
        )
        d = r * inv_x[s, :] + c_x[s, :] * d_last
        p_x[s, :] = d
        return q, d

    q_end, ez_last = lax.fori_loop(0, nx, ez_forward, (zero_plane, zero_plane))
    sx_send[0, 0] = backward_sweep(nx, plane, zero_plane, c_x, p_x)
    sx_send[0, 1] = ez_last - q_end * 0.03125
    for k in range(1, n):
        x_copy(1, k, sx_send.at[0], sx_recv.at[0]).start()

    arrived(has_right, send_ey, ey_next)

    def ex_right(i, ey_after):
        i = nx - 1 - i
        s = plane(i)
        ey_here = fields[EY, s, :]
        p = fields[HZ, s, :] - 32.0 * (ey_after - ey_here)
        p1[s, :] = p
        coef = ce[s, :]
        rhs[s, :] = fields[EX, s, :] + coef * (
            b_y(p, 0.0) - 0.015625 * b_z(fields[HY, s, :])
        )
        return ey_here

    lax.fori_loop(0, nx, ex_right, ey_next[...])
    ex_first, ex_last = y_sweep()
    sy_send[0, 0] = ex_first
    sy_send[0, 1] = ex_last - p1[across(ny - 1), :] * 0.03125
    for k in range(1, m):
        y_copy(1, k, sy_send.at[0], sy_recv.at[0]).start()

    arrived(has_left, send_hz, hz_prev)

    def ey_one(i, hz_last):
        s = plane(i)
        hz_here = fields[HZ, s, :]
        ey1[s, :] = fields[EY, s, :] + ce[s, :] * (
            0.015625 * b_z(fields[HX, s, :]) - (hz_here - hz_last)
        )
        return hz_here

    lax.fori_loop(0, nx, ey_one, hz_prev[...])

    def reduce_matrix(me, count, wait, recv, own, one_ref, two_ref, coef, zero):
        def up(j, b):
            wait(j)
            rf = recv[j, 2]
            g = rf / (1.0 - b * recv[j, 0])
            one_ref[j] = g
            two_ref[j] = b
            return recv[j, 1] + g * b * rf

        b = lax.fori_loop(0, me, up, zero)

        def down(t, e):
            j = count - 1 - t
            wait(j)
            rf = recv[j, 2]
            h = rf / (1.0 - e * recv[j, 1])
            one_ref[j] = h
            two_ref[j] = e
            return recv[j, 0] + h * e * rf

        e = lax.fori_loop(0, count - 1 - me, down, zero)
        rf = own[2]
        one = 1.0 - b * own[0]
        two = 1.0 - e * own[1]
        scale = 1.0 / (one * two - (b * rf) * (e * rf))
        coef[0] = b
        coef[1] = e
        coef[2] = two * scale
        coef[3] = b * rf * scale
        coef[4] = e * rf * scale
        coef[5] = one * scale

    reduce_matrix(gx, n, lambda j: x_wait(0, mx_send, mx_recv, j),
                  mx_recv, mx_send, gx_one, gx_two, coef_x, zero_plane)
    reduce_matrix(gy, m, lambda j: y_wait(0, my_send, my_recv, j),
                  my_recv, my_send, gy_one, gy_two, coef_y, zero_row)

    def reduce_sides(me, count, wait, recv, own, one_ref, two_ref, coef, zero):
        def up(j, a):
            wait(j)
            return recv[j, 1] + one_ref[j] * (a + two_ref[j] * recv[j, 0])

        a = lax.fori_loop(0, me, up, zero)

        def down(t, c):
            j = count - 1 - t
            wait(j)
            return recv[j, 0] + one_ref[j] * (c + two_ref[j] * recv[j, 1])

        c = lax.fori_loop(0, count - 1 - me, down, zero)
        a = a + coef[0] * own[0]
        c = c + coef[1] * own[1]
        return coef[2] * a + coef[3] * c, coef[4] * a + coef[5] * c

    def x_sides(step):
        return reduce_sides(
            gx, n, lambda j: x_wait(1 + step, sx_send.at[step], sx_recv.at[step], j),
            sx_recv.at[step], sx_send.at[step], gx_one, gx_two, coef_x, zero_plane)

    def y_sides(step):
        return reduce_sides(
            gy, m, lambda j: y_wait(1 + step, sy_send.at[step], sy_recv.at[step], j),
            sy_recv.at[step], sy_send.at[step], gy_one, gy_two, coef_y, zero_row)

    wl, wr = x_sides(0)
    wr_x[...] = wr

    def ez_fill(i, _):
        s = plane(i)
        ez1[s, :] = p_x[s, :] + l_x[s, :] * wl + r_x[s, :] * wr
        return 0

    lax.fori_loop(0, nx, ez_fill, 0)
    ez_send[...] = ez1[across(0), :]
    start(has_low, send_ez)

    wl, wr = y_sides(0)
    wr_y[...] = wr

    def ex_fill(j, _):
        s = row(j)
        ex1[across(j), :] = p_y[s, :] + l_y[s, :] * wl + r_y[s, :] * wr
        return 0

    lax.fori_loop(0, ny, ex_fill, 0)

    def v_right(i, _):
        s = plane(i)
        g = f_z(ey1[s, :])
        rhs[s, :] = (
            3.0 * ez1[s, :] - fields[EZ, s, :] - ce[s, :] * b_y(g, 0.0)
        )
        out[HX, s, :] = fields[HX, s, :] + g
        return 0

    lax.fori_loop(0, nx, v_right, 0)
    v_first, v_last = y_sweep()
    sy_send[1, 0] = v_first
    sy_send[1, 1] = v_last + 0.03125 * (
        out[HX, across(ny - 1), :] - fields[HX, across(ny - 1), :]
    )
    for k in range(1, m):
        y_copy(2, k, sy_send.at[1], sy_recv.at[1]).start()

    arrived(has_high, send_ez, ez_next)

    def ey_forward(i, carry):
        p_last, d_last = carry
        s = plane(i)
        one = pl.ds(i, 1)
        p = p1[s, :] + 64.0 * f_y(ex1[s, :], wr_y[one, :])
        p2[s, :] = p
        ey = ey1[s, :]
        hx = fields[HX, s, :] - 32.0 * f_y(ez1[s, :], ez_next[one, :]) + 0.5 * f_z(ey)
        r = ey + ce[s, :] * (0.015625 * b_z(hx) - (p - p_last))
        d = r * inv_x[s, :] + c_x[s, :] * d_last
        p_x[s, :] = d
        return p, d

    p_end, ey_last = lax.fori_loop(0, nx, ey_forward, (zero_plane, zero_plane))
    sx_send[1, 0] = backward_sweep(nx, plane, zero_plane, c_x, p_x)
    sx_send[1, 1] = ey_last + p_end * 0.03125
    for k in range(1, n):
        x_copy(2, k, sx_send.at[1], sx_recv.at[1]).start()

    def ex_two(i, ez_after):
        i = nx - 1 - i
        s = plane(i)
        ex = fields[EX, s, :]
        ez_here = ez1[s, :]
        d_ex = 0.5 * f_z(ex)
        change = d_ex - 32.0 * (ez_after - ez_here)
        two = 2.0 * ex1[s, :] - ex + (0.015625 * ce[s, :]) * b_z(change)
        out[EX, s, :] = two
        out[HY, s, :] = fields[HY, s, :] - d_ex - 0.5 * f_z(two)
        return ez_here

    lax.fori_loop(0, nx, ex_two, wr_x[...])

    wl, wr = y_sides(1)
    wr_y[...] = wr

    def v_fill(j, _):
        s = row(j)
        rhs[across(j), :] = p_y[s, :] + l_y[s, :] * wl + r_y[s, :] * wr
        return 0

    lax.fori_loop(0, ny, v_fill, 0)
    start(has_left, send_v)

    def last_ez(i, _):
        s = plane(i)
        v = rhs[s, :]
        out[EZ, s, :] = v - ez1[s, :]
        out[HX, s, :] = out[HX, s, :] - 32.0 * f_y(v, wr_y[pl.ds(i, 1), :])
        return 0

    lax.fori_loop(0, nx, last_ez, 0)

    wl, wr = x_sides(1)

    def last_ey(t, after):
        s = plane(nx - 1 - t)
        w = p_x[s, :] + l_x[s, :] * wl + r_x[s, :] * wr
        out[EY, s, :] = w
        out[HZ, s, :] = p2[s, :] - 32.0 * (after - w)
        return w

    lax.fori_loop(0, nx, last_ey, wr)

    arrived(has_right, send_v, v_next)

    def last_hy(t, after):
        s = plane(nx - 1 - t)
        v = rhs[s, :]
        out[HY, s, :] = out[HY, s, :] + 32.0 * (after - v)
        return v

    lax.fori_loop(0, nx, last_hy, v_next[...])

    sent(has_left, send_ey)
    sent(has_right, send_hz)
    sent(has_high, send_hx)
    sent(has_low, send_ez)
    sent(has_left, send_v)
    for k in range(1, n):
        x_copy(0, k, mx_send, mx_recv).wait_send()
        x_copy(1, k, sx_send.at[0], sx_recv.at[0]).wait_send()
        x_copy(2, k, sx_send.at[1], sx_recv.at[1]).wait_send()
    for k in range(1, m):
        y_copy(0, k, my_send, my_recv).wait_send()
        y_copy(1, k, sy_send.at[0], sy_recv.at[0]).wait_send()
        y_copy(2, k, sy_send.at[1], sy_recv.at[1]).wait_send()


def local(n, m, fields, region, eps_table):
    _, nx, ny, nz = fields.shape
    cells = nx * ny
    labels = eps_table.shape[0]
    big = pltpu.VMEM((cells, nz), jnp.float32)
    x_row = pltpu.VMEM((ny, nz), jnp.float32)
    y_row = pltpu.VMEM((nx, nz), jnp.float32)

    def sided(width, count):
        return [
            pltpu.VMEM((3, width, nz), jnp.float32),
            pltpu.VMEM((count, 3, width, nz), jnp.float32),
            pltpu.VMEM((count, width, nz), jnp.float32),
            pltpu.VMEM((count, width, nz), jnp.float32),
            pltpu.VMEM((6, width, nz), jnp.float32),
            pltpu.VMEM((2, 2, width, nz), jnp.float32),
            pltpu.VMEM((2, count, 2, width, nz), jnp.float32),
        ]

    vmem = pl.BlockSpec(memory_space=pltpu.VMEM)
    result = pl.pallas_call(
        functools.partial(kernel, n, m, nx, ny, nz, labels),
        out_shape=jax.ShapeDtypeStruct((6, cells, nz), jnp.float32),
        in_specs=[vmem, vmem, pl.BlockSpec(memory_space=pltpu.SMEM)],
        out_specs=vmem,
        scratch_shapes=[big] * 17
        + [x_row, x_row, y_row, y_row, y_row, y_row, x_row, x_row, y_row]
        + sided(ny, n)
        + sided(nx, m)
        + [
            pltpu.SemaphoreType.DMA((5,)),
            pltpu.SemaphoreType.DMA((5,)),
            pltpu.SemaphoreType.DMA((3, n)),
            pltpu.SemaphoreType.DMA((3, n)),
            pltpu.SemaphoreType.DMA((3, m)),
            pltpu.SemaphoreType.DMA((3, m)),
        ],
        compiler_params=pltpu.CompilerParams(
            collective_id=0, has_side_effects=True, vmem_limit_bytes=40 * 1024 * 1024
        ),
    )(fields.reshape(6, cells, nz), region.reshape(cells, nz), eps_table)
    return result.reshape(fields.shape)


def solution(mesh):
    return jax.shard_map(
        functools.partial(local, mesh.shape["gx"], mesh.shape["gy"]),
        mesh=mesh,
        in_specs=(P(None, "gx", "gy", None), P("gx", "gy", None), P()),
        out_specs=P(None, "gx", "gy", None),
        check_vma=False,
    )
```

```python
import functools

import jax
import jax.numpy as jnp
from jax import lax
from jax.experimental import pallas as pl
from jax.experimental.pallas import tpu as pltpu
from jax.sharding import PartitionSpec as P

MESH = pl.DeviceIdType.MESH
EX, EY, EZ, HX, HY, HZ = range(6)


def kernel(
    n, m, nx, ny, nz, labels,
    fields, region, eps, out,
    ce, small_k, inv_x, c_x, l_x, r_x, inv_y, c_y, l_y, r_y,
    p_x, p_y, rhs, p1, ey1, ez1, ex1, p2,
    ey_next, hz_prev, hx_prev, hx_send, ez_next, ez_send, v_next, wr_x, wr_y,
    mx_send, mx_recv, gx_one, gx_two, coef_x, sx_send, sx_recv,
    my_send, my_recv, gy_one, gy_two, coef_y, sy_send, sy_recv,
    near_send, near_recv, x_send, x_recv, y_send, y_recv,
):
    gx = lax.axis_index("gx")
    gy = lax.axis_index("gy")

    barrier = pltpu.get_barrier_semaphore()
    for k in range(1, n):
        pl.semaphore_signal(
            barrier, inc=1, device_id={"gx": lax.rem(gx + k, n)}, device_id_type=MESH
        )
    for k in range(1, m):
        pl.semaphore_signal(
            barrier, inc=1, device_id={"gy": lax.rem(gy + k, m)}, device_id_type=MESH
        )

    def plane(i):
        return pl.ds(pl.multiple_of(i * ny, ny), ny)

    def row(j):
        return pl.ds(pl.multiple_of(j * nx, nx), nx)

    def across(j):
        return pl.ds(j, nx, stride=ny)

    def loop(count, body, init):
        return lax.fori_loop(0, count, body, init, unroll=4)

    lane = lax.broadcasted_iota(jnp.int32, (ny, nz), 1)
    sub = lax.broadcasted_iota(jnp.int32, (ny, nz), 0)
    zero_plane = jnp.zeros((ny, nz), jnp.float32)
    zero_row = jnp.zeros((nx, nz), jnp.float32)

    def f_z(v):
        return jnp.where(lane == nz - 1, 0.0, pltpu.roll(v, nz - 1, 1)) - v

    def b_z(v):
        return v - jnp.where(lane == 0, 0.0, pltpu.roll(v, 1, 1))

    def f_y(v, after):
        return jnp.where(sub == ny - 1, after, pltpu.roll(v, ny - 1, 0)) - v

    def b_y(v, before):
        return v - jnp.where(sub == 0, before, pltpu.roll(v, 1, 0))

    def near(src, dst, slot, device):
        return pltpu.make_async_remote_copy(
            src_ref=src, dst_ref=dst, send_sem=near_send.at[slot],
            recv_sem=near_recv.at[slot], device_id=device, device_id_type=MESH,
        )

    to_left = {"gx": jnp.maximum(gx - 1, 0)}
    to_right = {"gx": jnp.minimum(gx + 1, n - 1)}
    to_low = {"gy": jnp.maximum(gy - 1, 0)}
    to_high = {"gy": jnp.minimum(gy + 1, m - 1)}
    send_ey = near(fields.at[EY, pl.ds(0, ny)], ey_next, 0, to_left)
    send_hz = near(fields.at[HZ, pl.ds((nx - 1) * ny, ny)], hz_prev, 1, to_right)
    send_hx = near(hx_send, hx_prev, 2, to_high)
    send_ez = near(ez_send, ez_next, 3, to_low)
    send_v = near(rhs.at[pl.ds(0, ny)], v_next, 4, to_left)

    has_left = gx > 0
    has_right = gx < n - 1
    has_low = gy > 0
    has_high = gy < m - 1

    def start(cond, copy):
        @pl.when(cond)
        def _():
            copy.start()

    def sent(cond, copy):
        @pl.when(cond)
        def _():
            copy.wait_send()

    def arrived(cond, copy, ref):
        @pl.when(cond)
        def _():
            copy.wait_recv()

        @pl.when(jnp.logical_not(cond))
        def _():
            ref[...] = jnp.zeros(ref.shape, jnp.float32)

    hx_send[...] = fields[HX, across(ny - 1), :]

    def x_copy(kind, k, src, dst):
        target = lax.rem(gx + k, n)
        return pltpu.make_async_remote_copy(
            src_ref=src, dst_ref=dst.at[gx], send_sem=x_send.at[kind, k],
            recv_sem=x_recv.at[kind, gx], device_id={"gx": target}, device_id_type=MESH,
        )

    def y_copy(kind, k, src, dst):
        target = lax.rem(gy + k, m)
        return pltpu.make_async_remote_copy(
            src_ref=src, dst_ref=dst.at[gy], send_sem=y_send.at[kind, k],
            recv_sem=y_recv.at[kind, gy], device_id={"gy": target}, device_id_type=MESH,
        )

    def x_wait(kind, src, dst, j):
        pltpu.make_async_remote_copy(
            src_ref=src, dst_ref=dst.at[j], send_sem=x_send.at[kind, 0],
            recv_sem=x_recv.at[kind, j], device_id={"gx": j}, device_id_type=MESH,
        ).wait_recv()

    def y_wait(kind, src, dst, j):
        pltpu.make_async_remote_copy(
            src_ref=src, dst_ref=dst.at[j], send_sem=y_send.at[kind, 0],
            recv_sem=y_recv.at[kind, j], device_id={"gy": j}, device_id_type=MESH,
        ).wait_recv()

    pl.semaphore_wait(barrier, n + m - 2)
    start(has_left, send_ey)
    start(has_high, send_hx)
    start(has_right, send_hz)

    def pick(label, lowest, width):
        if width == 1:
            return eps[lowest]
        half = width // 2
        return jnp.where(
            (label & half) != 0,
            pick(label, lowest + half, half),
            pick(label, lowest, half),
        )

    def coefficients(i, _):
        s = plane(i)
        label = region[s, :]
        eps_here = pick(label, 0, labels)
        small_k[s, :] = eps_here * (1.0 / 1024.0)
        ce[s, :] = 32.0 / eps_here
        return 0

    loop(nx, coefficients, 0)

    def factor(count, load_small, at, first, zero, inv_ref, c_ref, l_ref, r_ref, send_ref):
        ones = zero + 1.0

        def forward(i, carry):
            gap, d_last = carry
            small = load_small(i)
            total = small + gap
            c = 1.0 / (1.0 + total)
            d = c * d_last
            s = at(i)
            inv_ref[s, :] = c * small
            c_ref[s, :] = c
            l_ref[s, :] = d
            return total * c, d

        loop(count, forward, (zero + jnp.where(first, 0.0, 1.0), ones))

        def backward(t, carry):
            l_after, r_after = carry
            s = at(count - 1 - t)
            c = c_ref[s, :]
            l = l_ref[s, :] + c * l_after
            r = c * r_after
            l_ref[s, :] = l
            r_ref[s, :] = r
            return l, r

        l_first, r_first = loop(count, backward, (zero, ones))
        send_ref[0] = l_first
        send_ref[1] = r_ref[at(count - 1), :]
        send_ref[2] = r_first

    factor(nx, lambda i: small_k[plane(i), :], plane, gx == 0, zero_plane,
           inv_x, c_x, l_x, r_x, mx_send)
    for k in range(1, n):
        x_copy(0, k, mx_send, mx_recv).start()
    factor(ny, lambda j: small_k[across(j), :], row, gy == 0, zero_row,
           inv_y, c_y, l_y, r_y, my_send)
    for k in range(1, m):
        y_copy(0, k, my_send, my_recv).start()

    def backward_sweep(count, at, zero, c_ref, p_ref):
        def body(t, after):
            s = at(count - 1 - t)
            w = p_ref[s, :] + c_ref[s, :] * after
            p_ref[s, :] = w
            return w

        return loop(count, body, zero)

    def y_sweep():
        def body(j, last):
            s = row(j)
            d = rhs[across(j), :] * inv_y[s, :] + c_y[s, :] * last
            p_y[s, :] = d
            return d

        last = loop(ny, body, zero_row)
        return backward_sweep(ny, row, zero_row, c_y, p_y), last

    arrived(has_low, send_hx, hx_prev)

    def ez_forward(i, carry):
        q_last, d_last = carry
        s = plane(i)
        q = fields[HY, s, :] - 0.5 * f_z(fields[EX, s, :])
        coef = ce[s, :]
        r = fields[EZ, s, :] + coef * (
            (q - q_last) - b_y(fields[HX, s, :], hx_prev[pl.ds(i, 1), :])
        )
        d = r * inv_x[s, :] + c_x[s, :] * d_last
        p_x[s, :] = d
        return q, d

    q_end, ez_last = loop(nx, ez_forward, (zero_plane, zero_plane))
    sx_send[0, 0] = backward_sweep(nx, plane, zero_plane, c_x, p_x)
    sx_send[0, 1] = ez_last - q_end * 0.03125
    for k in range(1, n):
        x_copy(1, k, sx_send.at[0], sx_recv.at[0]).start()

    arrived(has_right, send_ey, ey_next)

    def ex_right(i, ey_after):
        i = nx - 1 - i
        s = plane(i)
        ey_here = fields[EY, s, :]
        p = fields[HZ, s, :] - 32.0 * (ey_after - ey_here)
        p1[s, :] = p
        coef = ce[s, :]
        rhs[s, :] = fields[EX, s, :] + coef * (
            b_y(p, 0.0) - 0.015625 * b_z(fields[HY, s, :])
        )
        return ey_here

    loop(nx, ex_right, ey_next[...])
    ex_first, ex_last = y_sweep()
    sy_send[0, 0] = ex_first
    sy_send[0, 1] = ex_last - p1[across(ny - 1), :] * 0.03125
    for k in range(1, m):
        y_copy(1, k, sy_send.at[0], sy_recv.at[0]).start()

    arrived(has_left, send_hz, hz_prev)

    def ey_one(i, hz_last):
        s = plane(i)
        hz_here = fields[HZ, s, :]
        ey1[s, :] = fields[EY, s, :] + ce[s, :] * (
            0.015625 * b_z(fields[HX, s, :]) - (hz_here - hz_last)
        )
        return hz_here

    loop(nx, ey_one, hz_prev[...])

    def reduce_matrix(me, count, wait, recv, own, one_ref, two_ref, coef, zero):
        def up(j, b):
            wait(j)
            rf = recv[j, 2]
            g = rf / (1.0 - b * recv[j, 0])
            one_ref[j] = g
            two_ref[j] = b
            return recv[j, 1] + g * b * rf

        b = lax.fori_loop(0, me, up, zero)

        def down(t, e):
            j = count - 1 - t
            wait(j)
            rf = recv[j, 2]
            h = rf / (1.0 - e * recv[j, 1])
            one_ref[j] = h
            two_ref[j] = e
            return recv[j, 0] + h * e * rf

        e = lax.fori_loop(0, count - 1 - me, down, zero)
        rf = own[2]
        one = 1.0 - b * own[0]
        two = 1.0 - e * own[1]
        scale = 1.0 / (one * two - (b * rf) * (e * rf))
        coef[0] = b
        coef[1] = e
        coef[2] = two * scale
        coef[3] = b * rf * scale
        coef[4] = e * rf * scale
        coef[5] = one * scale

    reduce_matrix(gx, n, lambda j: x_wait(0, mx_send, mx_recv, j),
                  mx_recv, mx_send, gx_one, gx_two, coef_x, zero_plane)
    reduce_matrix(gy, m, lambda j: y_wait(0, my_send, my_recv, j),
                  my_recv, my_send, gy_one, gy_two, coef_y, zero_row)

    def reduce_sides(me, count, wait, recv, own, one_ref, two_ref, coef, zero):
        def up(j, a):
            wait(j)
            return recv[j, 1] + one_ref[j] * (a + two_ref[j] * recv[j, 0])

        a = lax.fori_loop(0, me, up, zero)

        def down(t, c):
            j = count - 1 - t
            wait(j)
            return recv[j, 0] + one_ref[j] * (c + two_ref[j] * recv[j, 1])

        c = lax.fori_loop(0, count - 1 - me, down, zero)
        a = a + coef[0] * own[0]
        c = c + coef[1] * own[1]
        return coef[2] * a + coef[3] * c, coef[4] * a + coef[5] * c

    def x_sides(step):
        return reduce_sides(
            gx, n, lambda j: x_wait(1 + step, sx_send.at[step], sx_recv.at[step], j),
            sx_recv.at[step], sx_send.at[step], gx_one, gx_two, coef_x, zero_plane)

    def y_sides(step):
        return reduce_sides(
            gy, m, lambda j: y_wait(1 + step, sy_send.at[step], sy_recv.at[step], j),
            sy_recv.at[step], sy_send.at[step], gy_one, gy_two, coef_y, zero_row)

    wl, wr = x_sides(0)
    wr_x[...] = wr

    def ez_fill(i, _):
        s = plane(i)
        ez1[s, :] = p_x[s, :] + l_x[s, :] * wl + r_x[s, :] * wr
        return 0

    loop(nx, ez_fill, 0)
    ez_send[...] = ez1[across(0), :]
    start(has_low, send_ez)

    wl, wr = y_sides(0)
    wr_y[...] = wr

    def ex_fill(j, _):
        s = row(j)
        ex1[across(j), :] = p_y[s, :] + l_y[s, :] * wl + r_y[s, :] * wr
        return 0

    loop(ny, ex_fill, 0)

    def v_right(i, _):
        s = plane(i)
        g = f_z(ey1[s, :])
        rhs[s, :] = (
            3.0 * ez1[s, :] - fields[EZ, s, :] - ce[s, :] * b_y(g, 0.0)
        )
        out[HX, s, :] = fields[HX, s, :] + g
        return 0

    loop(nx, v_right, 0)
    v_first, v_last = y_sweep()
    sy_send[1, 0] = v_first
    sy_send[1, 1] = v_last + 0.03125 * (
        out[HX, across(ny - 1), :] - fields[HX, across(ny - 1), :]
    )
    for k in range(1, m):
        y_copy(2, k, sy_send.at[1], sy_recv.at[1]).start()

    arrived(has_high, send_ez, ez_next)

    def ey_forward(i, carry):
        p_last, d_last = carry
        s = plane(i)
        one = pl.ds(i, 1)
        p = p1[s, :] + 64.0 * f_y(ex1[s, :], wr_y[one, :])
        p2[s, :] = p
        ey = ey1[s, :]
        hx = fields[HX, s, :] - 32.0 * f_y(ez1[s, :], ez_next[one, :]) + 0.5 * f_z(ey)
        r = ey + ce[s, :] * (0.015625 * b_z(hx) - (p - p_last))
        d = r * inv_x[s, :] + c_x[s, :] * d_last
        p_x[s, :] = d
        return p, d

    p_end, ey_last = loop(nx, ey_forward, (zero_plane, zero_plane))
    sx_send[1, 0] = backward_sweep(nx, plane, zero_plane, c_x, p_x)
    sx_send[1, 1] = ey_last + p_end * 0.03125
    for k in range(1, n):
        x_copy(2, k, sx_send.at[1], sx_recv.at[1]).start()

    def ex_two(i, ez_after):
        i = nx - 1 - i
        s = plane(i)
        ex = fields[EX, s, :]
        ez_here = ez1[s, :]
        d_ex = 0.5 * f_z(ex)
        change = d_ex - 32.0 * (ez_after - ez_here)
        two = 2.0 * ex1[s, :] - ex + (0.015625 * ce[s, :]) * b_z(change)
        out[EX, s, :] = two
        out[HY, s, :] = fields[HY, s, :] - d_ex - 0.5 * f_z(two)
        return ez_here

    loop(nx, ex_two, wr_x[...])

    wl, wr = y_sides(1)
    wr_y[...] = wr

    def v_fill(j, _):
        s = row(j)
        rhs[across(j), :] = p_y[s, :] + l_y[s, :] * wl + r_y[s, :] * wr
        return 0

    loop(ny, v_fill, 0)
    start(has_left, send_v)

    def last_ez(i, _):
        s = plane(i)
        v = rhs[s, :]
        out[EZ, s, :] = v - ez1[s, :]
        out[HX, s, :] = out[HX, s, :] - 32.0 * f_y(v, wr_y[pl.ds(i, 1), :])
        return 0

    loop(nx, last_ez, 0)

    wl, wr = x_sides(1)

    def last_ey(t, after):
        s = plane(nx - 1 - t)
        w = p_x[s, :] + l_x[s, :] * wl + r_x[s, :] * wr
        out[EY, s, :] = w
        out[HZ, s, :] = p2[s, :] - 32.0 * (after - w)
        return w

    loop(nx, last_ey, wr)

    arrived(has_right, send_v, v_next)

    def last_hy(t, after):
        s = plane(nx - 1 - t)
        v = rhs[s, :]
        out[HY, s, :] = out[HY, s, :] + 32.0 * (after - v)
        return v

    loop(nx, last_hy, v_next[...])

    sent(has_left, send_ey)
    sent(has_right, send_hz)
    sent(has_high, send_hx)
    sent(has_low, send_ez)
    sent(has_left, send_v)
    for k in range(1, n):
        x_copy(0, k, mx_send, mx_recv).wait_send()
        x_copy(1, k, sx_send.at[0], sx_recv.at[0]).wait_send()
        x_copy(2, k, sx_send.at[1], sx_recv.at[1]).wait_send()
    for k in range(1, m):
        y_copy(0, k, my_send, my_recv).wait_send()
        y_copy(1, k, sy_send.at[0], sy_recv.at[0]).wait_send()
        y_copy(2, k, sy_send.at[1], sy_recv.at[1]).wait_send()


def local(n, m, fields, region, eps_table):
    _, nx, ny, nz = fields.shape
    cells = nx * ny
    labels = eps_table.shape[0]
    big = pltpu.VMEM((cells, nz), jnp.float32)
    x_row = pltpu.VMEM((ny, nz), jnp.float32)
    y_row = pltpu.VMEM((nx, nz), jnp.float32)

    def sided(width, count):
        return [
            pltpu.VMEM((3, width, nz), jnp.float32),
            pltpu.VMEM((count, 3, width, nz), jnp.float32),
            pltpu.VMEM((count, width, nz), jnp.float32),
            pltpu.VMEM((count, width, nz), jnp.float32),
            pltpu.VMEM((6, width, nz), jnp.float32),
            pltpu.VMEM((2, 2, width, nz), jnp.float32),
            pltpu.VMEM((2, count, 2, width, nz), jnp.float32),
        ]

    vmem = pl.BlockSpec(memory_space=pltpu.VMEM)
    result = pl.pallas_call(
        functools.partial(kernel, n, m, nx, ny, nz, labels),
        out_shape=jax.ShapeDtypeStruct((6, cells, nz), jnp.float32),
        in_specs=[vmem, vmem, pl.BlockSpec(memory_space=pltpu.SMEM)],
        out_specs=vmem,
        scratch_shapes=[big] * 18
        + [x_row, x_row, y_row, y_row, y_row, y_row, x_row, x_row, y_row]
        + sided(ny, n)
        + sided(nx, m)
        + [
            pltpu.SemaphoreType.DMA((5,)),
            pltpu.SemaphoreType.DMA((5,)),
            pltpu.SemaphoreType.DMA((3, n)),
            pltpu.SemaphoreType.DMA((3, n)),
            pltpu.SemaphoreType.DMA((3, m)),
            pltpu.SemaphoreType.DMA((3, m)),
        ],
        compiler_params=pltpu.CompilerParams(
            collective_id=0, has_side_effects=True, vmem_limit_bytes=40 * 1024 * 1024
        ),
    )(fields.reshape(6, cells, nz), region.reshape(cells, nz), eps_table)
    return result.reshape(fields.shape)


def solution(mesh):
    return jax.shard_map(
        functools.partial(local, mesh.shape["gx"], mesh.shape["gy"]),
        mesh=mesh,
        in_specs=(P(None, "gx", "gy", None), P("gx", "gy", None), P()),
        out_specs=P(None, "gx", "gy", None),
        check_vma=False,
    )
```

```python
import functools

import jax
import jax.numpy as jnp
from jax import lax
from jax.experimental import pallas as pl
from jax.experimental.pallas import tpu as pltpu
from jax.sharding import PartitionSpec as P

MESH = pl.DeviceIdType.MESH
EX, EY, EZ, HX, HY, HZ = range(6)


def kernel(
    n, m, nx, ny, nz, labels,
    fields_in, region_in, eps_in, out, fields, region, eps,
    ce, small_k, inv_x, c_x, l_x, r_x, inv_y, c_y, l_y, r_y,
    p_x, p_y, rhs, p1, ey1, ez1, ex1, p2,
    ey_next, hz_prev, hx_prev, hx_send, ez_next, ez_send, v_next, wr_x, wr_y,
    mx_send, mx_recv, gx_one, gx_two, coef_x, sx_send, sx_recv,
    my_send, my_recv, gy_one, gy_two, coef_y, sy_send, sy_recv,
    load_sem, near_send, near_recv, x_send, x_recv, y_send, y_recv,
):
    gx = lax.axis_index("gx")
    gy = lax.axis_index("gy")

    load_eps = pltpu.make_async_copy(eps_in, eps, load_sem.at[7])
    load_region = pltpu.make_async_copy(region_in, region, load_sem.at[6])
    loads = [
        pltpu.make_async_copy(fields_in.at[f], fields.at[f], load_sem.at[f]) for f in range(6)
    ]
    barrier = pltpu.get_barrier_semaphore()
    load_eps.start()
    load_region.start()
    for f in (HX, EY, HZ, EX, HY, EZ):
        loads[f].start()
    for k in range(1, n):
        pl.semaphore_signal(
            barrier, inc=1, device_id={"gx": lax.rem(gx + k, n)}, device_id_type=MESH
        )
    for k in range(1, m):
        pl.semaphore_signal(
            barrier, inc=1, device_id={"gy": lax.rem(gy + k, m)}, device_id_type=MESH
        )

    def plane(i):
        return pl.ds(pl.multiple_of(i * ny, ny), ny)

    def row(j):
        return pl.ds(pl.multiple_of(j * nx, nx), nx)

    def across(j):
        return pl.ds(j, nx, stride=ny)

    def loop(count, body, init):
        return lax.fori_loop(0, count, body, init, unroll=4)

    lane = lax.broadcasted_iota(jnp.int32, (ny, nz), 1)
    sub = lax.broadcasted_iota(jnp.int32, (ny, nz), 0)
    zero_plane = jnp.zeros((ny, nz), jnp.float32)
    zero_row = jnp.zeros((nx, nz), jnp.float32)

    def f_z(v):
        return jnp.where(lane == nz - 1, 0.0, pltpu.roll(v, nz - 1, 1)) - v

    def b_z(v):
        return v - jnp.where(lane == 0, 0.0, pltpu.roll(v, 1, 1))

    def f_y(v, after):
        return jnp.where(sub == ny - 1, after, pltpu.roll(v, ny - 1, 0)) - v

    def b_y(v, before):
        return v - jnp.where(sub == 0, before, pltpu.roll(v, 1, 0))

    def near(src, dst, slot, device):
        return pltpu.make_async_remote_copy(
            src_ref=src, dst_ref=dst, send_sem=near_send.at[slot],
            recv_sem=near_recv.at[slot], device_id=device, device_id_type=MESH,
        )

    to_left = {"gx": jnp.maximum(gx - 1, 0)}
    to_right = {"gx": jnp.minimum(gx + 1, n - 1)}
    to_low = {"gy": jnp.maximum(gy - 1, 0)}
    to_high = {"gy": jnp.minimum(gy + 1, m - 1)}
    send_ey = near(fields.at[EY, pl.ds(0, ny)], ey_next, 0, to_left)
    send_hz = near(fields.at[HZ, pl.ds((nx - 1) * ny, ny)], hz_prev, 1, to_right)
    send_hx = near(hx_send, hx_prev, 2, to_high)
    send_ez = near(ez_send, ez_next, 3, to_low)
    send_v = near(rhs.at[pl.ds(0, ny)], v_next, 4, to_left)

    has_left = gx > 0
    has_right = gx < n - 1
    has_low = gy > 0
    has_high = gy < m - 1

    def start(cond, copy):
        @pl.when(cond)
        def _():
            copy.start()

    def sent(cond, copy):
        @pl.when(cond)
        def _():
            copy.wait_send()

    def arrived(cond, copy, ref):
        @pl.when(cond)
        def _():
            copy.wait_recv()

        @pl.when(jnp.logical_not(cond))
        def _():
            ref[...] = jnp.zeros(ref.shape, jnp.float32)


    def x_copy(kind, k, src, dst):
        target = lax.rem(gx + k, n)
        return pltpu.make_async_remote_copy(
            src_ref=src, dst_ref=dst.at[gx], send_sem=x_send.at[kind, k],
            recv_sem=x_recv.at[kind, gx], device_id={"gx": target}, device_id_type=MESH,
        )

    def y_copy(kind, k, src, dst):
        target = lax.rem(gy + k, m)
        return pltpu.make_async_remote_copy(
            src_ref=src, dst_ref=dst.at[gy], send_sem=y_send.at[kind, k],
            recv_sem=y_recv.at[kind, gy], device_id={"gy": target}, device_id_type=MESH,
        )

    def x_wait(kind, src, dst, j):
        pltpu.make_async_remote_copy(
            src_ref=src, dst_ref=dst.at[j], send_sem=x_send.at[kind, 0],
            recv_sem=x_recv.at[kind, j], device_id={"gx": j}, device_id_type=MESH,
        ).wait_recv()

    def y_wait(kind, src, dst, j):
        pltpu.make_async_remote_copy(
            src_ref=src, dst_ref=dst.at[j], send_sem=y_send.at[kind, 0],
            recv_sem=y_recv.at[kind, j], device_id={"gy": j}, device_id_type=MESH,
        ).wait_recv()

    def pick(label, lowest, width):
        if width == 1:
            return eps[lowest]
        half = width // 2
        return jnp.where(
            (label & half) != 0,
            pick(label, lowest + half, half),
            pick(label, lowest, half),
        )

    def coefficients(i, _):
        s = plane(i)
        label = region[s, :]
        eps_here = pick(label, 0, labels)
        small_k[s, :] = eps_here * (1.0 / 1024.0)
        ce[s, :] = 32.0 / eps_here
        return 0

    load_eps.wait()
    load_region.wait()
    loop(nx, coefficients, 0)
    pl.semaphore_wait(barrier, n + m - 2)
    loads[HX].wait()
    hx_send[...] = fields[HX, across(ny - 1), :]
    start(has_high, send_hx)
    loads[EY].wait()
    start(has_left, send_ey)
    loads[HZ].wait()
    start(has_right, send_hz)

    per = ny // nx

    def factor_step(small, carry, s, inv_ref, c_ref, l_ref):
        gap, d_last = carry
        total = small + gap
        c = 1.0 / (1.0 + total)
        d = c * d_last
        inv_ref[s, :] = c * small
        c_ref[s, :] = c
        l_ref[s, :] = d
        return total * c, d

    def factor_forward(i, carry):
        on_x, on_y = carry
        on_x = factor_step(small_k[plane(i), :], on_x, plane(i), inv_x, c_x, l_x)
        for k in range(per):
            j = i * per + k
            on_y = factor_step(small_k[across(j), :], on_y, row(j), inv_y, c_y, l_y)
        return on_x, on_y

    loop(nx, factor_forward, (
        (zero_plane + jnp.where(gx == 0, 0.0, 1.0), zero_plane + 1.0),
        (zero_row + jnp.where(gy == 0, 0.0, 1.0), zero_row + 1.0),
    ))

    def factor_back(carry, s, c_ref, l_ref, r_ref):
        l_after, r_after = carry
        c = c_ref[s, :]
        l = l_ref[s, :] + c * l_after
        r = c * r_after
        l_ref[s, :] = l
        r_ref[s, :] = r
        return l, r

    def factor_backward(t, carry):
        on_x, on_y = carry
        on_x = factor_back(on_x, plane(nx - 1 - t), c_x, l_x, r_x)
        for k in range(per):
            on_y = factor_back(on_y, row(ny - 1 - t * per - k), c_y, l_y, r_y)
        return on_x, on_y

    on_x, on_y = loop(
        nx, factor_backward, ((zero_plane, zero_plane + 1.0), (zero_row, zero_row + 1.0))
    )
    mx_send[0] = on_x[0]
    mx_send[1] = r_x[plane(nx - 1), :]
    mx_send[2] = on_x[1]
    for k in range(1, n):
        x_copy(0, k, mx_send, mx_recv).start()
    my_send[0] = on_y[0]
    my_send[1] = r_y[row(ny - 1), :]
    my_send[2] = on_y[1]
    for k in range(1, m):
        y_copy(0, k, my_send, my_recv).start()

    def backward_sweep(count, at, zero, c_ref, p_ref):
        def body(t, after):
            s = at(count - 1 - t)
            w = p_ref[s, :] + c_ref[s, :] * after
            p_ref[s, :] = w
            return w

        return loop(count, body, zero)

    def y_sweep():
        def body(j, last):
            s = row(j)
            d = rhs[across(j), :] * inv_y[s, :] + c_y[s, :] * last
            p_y[s, :] = d
            return d

        last = loop(ny, body, zero_row)
        return backward_sweep(ny, row, zero_row, c_y, p_y), last

    loads[EX].wait()
    loads[HY].wait()
    loads[EZ].wait()
    arrived(has_low, send_hx, hx_prev)

    def ez_forward(i, carry):
        q_last, d_last = carry
        s = plane(i)
        q = fields[HY, s, :] - 0.5 * f_z(fields[EX, s, :])
        coef = ce[s, :]
        r = fields[EZ, s, :] + coef * (
            (q - q_last) - b_y(fields[HX, s, :], hx_prev[pl.ds(i, 1), :])
        )
        d = r * inv_x[s, :] + c_x[s, :] * d_last
        p_x[s, :] = d
        return q, d

    q_end, ez_last = loop(nx, ez_forward, (zero_plane, zero_plane))
    sx_send[0, 0] = backward_sweep(nx, plane, zero_plane, c_x, p_x)
    sx_send[0, 1] = ez_last - q_end * 0.03125
    for k in range(1, n):
        x_copy(1, k, sx_send.at[0], sx_recv.at[0]).start()

    arrived(has_right, send_ey, ey_next)

    def ex_right(i, ey_after):
        i = nx - 1 - i
        s = plane(i)
        ey_here = fields[EY, s, :]
        p = fields[HZ, s, :] - 32.0 * (ey_after - ey_here)
        p1[s, :] = p
        coef = ce[s, :]
        rhs[s, :] = fields[EX, s, :] + coef * (
            b_y(p, 0.0) - 0.015625 * b_z(fields[HY, s, :])
        )
        return ey_here

    loop(nx, ex_right, ey_next[...])
    ex_first, ex_last = y_sweep()
    sy_send[0, 0] = ex_first
    sy_send[0, 1] = ex_last - p1[across(ny - 1), :] * 0.03125
    for k in range(1, m):
        y_copy(1, k, sy_send.at[0], sy_recv.at[0]).start()

    arrived(has_left, send_hz, hz_prev)

    def ey_one(i, hz_last):
        s = plane(i)
        hz_here = fields[HZ, s, :]
        ey1[s, :] = fields[EY, s, :] + ce[s, :] * (
            0.015625 * b_z(fields[HX, s, :]) - (hz_here - hz_last)
        )
        return hz_here

    loop(nx, ey_one, hz_prev[...])

    def reduce_matrix(me, count, wait, recv, own, one_ref, two_ref, coef, zero):
        def up(j, b):
            wait(j)
            rf = recv[j, 2]
            g = rf / (1.0 - b * recv[j, 0])
            one_ref[j] = g
            two_ref[j] = b
            return recv[j, 1] + g * b * rf

        b = lax.fori_loop(0, me, up, zero)

        def down(t, e):
            j = count - 1 - t
            wait(j)
            rf = recv[j, 2]
            h = rf / (1.0 - e * recv[j, 1])
            one_ref[j] = h
            two_ref[j] = e
            return recv[j, 0] + h * e * rf

        e = lax.fori_loop(0, count - 1 - me, down, zero)
        rf = own[2]
        one = 1.0 - b * own[0]
        two = 1.0 - e * own[1]
        scale = 1.0 / (one * two - (b * rf) * (e * rf))
        coef[0] = b
        coef[1] = e
        coef[2] = two * scale
        coef[3] = b * rf * scale
        coef[4] = e * rf * scale
        coef[5] = one * scale

    reduce_matrix(gx, n, lambda j: x_wait(0, mx_send, mx_recv, j),
                  mx_recv, mx_send, gx_one, gx_two, coef_x, zero_plane)
    reduce_matrix(gy, m, lambda j: y_wait(0, my_send, my_recv, j),
                  my_recv, my_send, gy_one, gy_two, coef_y, zero_row)

    def reduce_sides(me, count, wait, recv, own, one_ref, two_ref, coef, zero):
        def up(j, a):
            wait(j)
            return recv[j, 1] + one_ref[j] * (a + two_ref[j] * recv[j, 0])

        a = lax.fori_loop(0, me, up, zero)

        def down(t, c):
            j = count - 1 - t
            wait(j)
            return recv[j, 0] + one_ref[j] * (c + two_ref[j] * recv[j, 1])

        c = lax.fori_loop(0, count - 1 - me, down, zero)
        a = a + coef[0] * own[0]
        c = c + coef[1] * own[1]
        return coef[2] * a + coef[3] * c, coef[4] * a + coef[5] * c

    def x_sides(step):
        return reduce_sides(
            gx, n, lambda j: x_wait(1 + step, sx_send.at[step], sx_recv.at[step], j),
            sx_recv.at[step], sx_send.at[step], gx_one, gx_two, coef_x, zero_plane)

    def y_sides(step):
        return reduce_sides(
            gy, m, lambda j: y_wait(1 + step, sy_send.at[step], sy_recv.at[step], j),
            sy_recv.at[step], sy_send.at[step], gy_one, gy_two, coef_y, zero_row)

    wl, wr = x_sides(0)
    wr_x[...] = wr

    def ez_fill(i, _):
        s = plane(i)
        ez1[s, :] = p_x[s, :] + l_x[s, :] * wl + r_x[s, :] * wr
        return 0

    loop(nx, ez_fill, 0)
    ez_send[...] = ez1[across(0), :]
    start(has_low, send_ez)

    wl, wr = y_sides(0)
    wr_y[...] = wr

    def ex_fill(j, _):
        s = row(j)
        ex1[across(j), :] = p_y[s, :] + l_y[s, :] * wl + r_y[s, :] * wr
        return 0

    loop(ny, ex_fill, 0)

    def v_right(i, _):
        s = plane(i)
        g = f_z(ey1[s, :])
        rhs[s, :] = (
            3.0 * ez1[s, :] - fields[EZ, s, :] - ce[s, :] * b_y(g, 0.0)
        )
        out[HX, s, :] = fields[HX, s, :] + g
        return 0

    loop(nx, v_right, 0)
    v_first, v_last = y_sweep()
    sy_send[1, 0] = v_first
    sy_send[1, 1] = v_last + 0.03125 * (
        out[HX, across(ny - 1), :] - fields[HX, across(ny - 1), :]
    )
    for k in range(1, m):
        y_copy(2, k, sy_send.at[1], sy_recv.at[1]).start()

    arrived(has_high, send_ez, ez_next)

    def ey_forward(i, carry):
        p_last, d_last = carry
        s = plane(i)
        one = pl.ds(i, 1)
        p = p1[s, :] + 64.0 * f_y(ex1[s, :], wr_y[one, :])
        p2[s, :] = p
        ey = ey1[s, :]
        hx = fields[HX, s, :] - 32.0 * f_y(ez1[s, :], ez_next[one, :]) + 0.5 * f_z(ey)
        r = ey + ce[s, :] * (0.015625 * b_z(hx) - (p - p_last))
        d = r * inv_x[s, :] + c_x[s, :] * d_last
        p_x[s, :] = d
        return p, d

    p_end, ey_last = loop(nx, ey_forward, (zero_plane, zero_plane))
    sx_send[1, 0] = backward_sweep(nx, plane, zero_plane, c_x, p_x)
    sx_send[1, 1] = ey_last + p_end * 0.03125
    for k in range(1, n):
        x_copy(2, k, sx_send.at[1], sx_recv.at[1]).start()

    def ex_two(i, ez_after):
        i = nx - 1 - i
        s = plane(i)
        ex = fields[EX, s, :]
        ez_here = ez1[s, :]
        d_ex = 0.5 * f_z(ex)
        change = d_ex - 32.0 * (ez_after - ez_here)
        two = 2.0 * ex1[s, :] - ex + (0.015625 * ce[s, :]) * b_z(change)
        out[EX, s, :] = two
        out[HY, s, :] = fields[HY, s, :] - d_ex - 0.5 * f_z(two)
        return ez_here

    loop(nx, ex_two, wr_x[...])

    wl, wr = y_sides(1)
    wr_y[...] = wr

    def v_fill(j, _):
        s = row(j)
        rhs[across(j), :] = p_y[s, :] + l_y[s, :] * wl + r_y[s, :] * wr
        return 0

    loop(ny, v_fill, 0)
    start(has_left, send_v)

    def last_ez(i, _):
        s = plane(i)
        v = rhs[s, :]
        out[EZ, s, :] = v - ez1[s, :]
        out[HX, s, :] = out[HX, s, :] - 32.0 * f_y(v, wr_y[pl.ds(i, 1), :])
        return 0

    loop(nx, last_ez, 0)

    wl, wr = x_sides(1)

    def last_ey(t, after):
        s = plane(nx - 1 - t)
        w = p_x[s, :] + l_x[s, :] * wl + r_x[s, :] * wr
        out[EY, s, :] = w
        out[HZ, s, :] = p2[s, :] - 32.0 * (after - w)
        return w

    loop(nx, last_ey, wr)

    arrived(has_right, send_v, v_next)

    def last_hy(t, after):
        s = plane(nx - 1 - t)
        v = rhs[s, :]
        out[HY, s, :] = out[HY, s, :] + 32.0 * (after - v)
        return v

    loop(nx, last_hy, v_next[...])

    sent(has_left, send_ey)
    sent(has_right, send_hz)
    sent(has_high, send_hx)
    sent(has_low, send_ez)
    sent(has_left, send_v)
    for k in range(1, n):
        x_copy(0, k, mx_send, mx_recv).wait_send()
        x_copy(1, k, sx_send.at[0], sx_recv.at[0]).wait_send()
        x_copy(2, k, sx_send.at[1], sx_recv.at[1]).wait_send()
    for k in range(1, m):
        y_copy(0, k, my_send, my_recv).wait_send()
        y_copy(1, k, sy_send.at[0], sy_recv.at[0]).wait_send()
        y_copy(2, k, sy_send.at[1], sy_recv.at[1]).wait_send()


def local(n, m, fields, region, eps_table):
    _, nx, ny, nz = fields.shape
    cells = nx * ny
    labels = eps_table.shape[0]
    big = pltpu.VMEM((cells, nz), jnp.float32)
    x_row = pltpu.VMEM((ny, nz), jnp.float32)
    y_row = pltpu.VMEM((nx, nz), jnp.float32)

    def sided(width, count):
        return [
            pltpu.VMEM((3, width, nz), jnp.float32),
            pltpu.VMEM((count, 3, width, nz), jnp.float32),
            pltpu.VMEM((count, width, nz), jnp.float32),
            pltpu.VMEM((count, width, nz), jnp.float32),
            pltpu.VMEM((6, width, nz), jnp.float32),
            pltpu.VMEM((2, 2, width, nz), jnp.float32),
            pltpu.VMEM((2, count, 2, width, nz), jnp.float32),
        ]

    vmem = pl.BlockSpec(memory_space=pltpu.VMEM)
    result = pl.pallas_call(
        functools.partial(kernel, n, m, nx, ny, nz, labels),
        out_shape=pltpu.VMEM((6, cells, nz), jnp.float32),
        in_specs=[pl.BlockSpec(memory_space=pl.ANY)] * 3,
        out_specs=vmem,
        scratch_shapes=[
            pltpu.VMEM((6, cells, nz), jnp.float32),
            pltpu.VMEM((cells, nz), jnp.int32),
            pltpu.SMEM((labels,), jnp.float32),
        ]
        + [big] * 18
        + [x_row, x_row, y_row, y_row, y_row, y_row, x_row, x_row, y_row]
        + sided(ny, n)
        + sided(nx, m)
        + [
            pltpu.SemaphoreType.DMA((8,)),
            pltpu.SemaphoreType.DMA((5,)),
            pltpu.SemaphoreType.DMA((5,)),
            pltpu.SemaphoreType.DMA((3, n)),
            pltpu.SemaphoreType.DMA((3, n)),
            pltpu.SemaphoreType.DMA((3, m)),
            pltpu.SemaphoreType.DMA((3, m)),
        ],
        compiler_params=pltpu.CompilerParams(
            collective_id=0, has_side_effects=True, vmem_limit_bytes=60 * 1024 * 1024
        ),
    )(fields.reshape(6, cells, nz), region.reshape(cells, nz), eps_table)
    return result.reshape(fields.shape)


def solution(mesh):
    return jax.shard_map(
        functools.partial(local, mesh.shape["gx"], mesh.shape["gy"]),
        mesh=mesh,
        in_specs=(P(None, "gx", "gy", None), P("gx", "gy", None), P()),
        out_specs=P(None, "gx", "gy", None),
        check_vma=False,
    )
```

```python
import functools

import jax
import jax.numpy as jnp
from jax import lax
from jax.experimental import pallas as pl
from jax.experimental.pallas import tpu as pltpu
from jax.sharding import PartitionSpec as P

MESH = pl.DeviceIdType.MESH
EX, EY, EZ, HX, HY, HZ = range(6)


def kernel(
    n, m, nx, ny, nz, labels,
    fields_in, region_in, eps_in, out, fields, region, eps,
    ce, small_k, inv_x, c_x, l_x, r_x, inv_y, c_y, l_y, r_y,
    p_x, p_y, rhs, p1, ey1, ez1, ex1, p2,
    ey_next, hz_prev, hx_prev, hx_send, ez_next, ez_send, v_next, wr_x, wr_y,
    mx_send, mx_recv, gx_one, gx_two, coef_x, sx_send, sx_recv,
    my_send, my_recv, gy_one, gy_two, coef_y, sy_send, sy_recv,
    load_sem, near_send, near_recv, x_send, x_recv, y_send, y_recv,
):
    gx = lax.axis_index("gx")
    gy = lax.axis_index("gy")

    load_eps = pltpu.make_async_copy(eps_in, eps, load_sem.at[7])
    load_region = pltpu.make_async_copy(region_in, region, load_sem.at[6])
    loads = [
        pltpu.make_async_copy(fields_in.at[f], fields.at[f], load_sem.at[f]) for f in range(6)
    ]
    barrier = pltpu.get_barrier_semaphore()
    load_eps.start()
    load_region.start()
    for f in (HX, EY, HZ, EX, HY, EZ):
        loads[f].start()
    for k in range(1, n):
        pl.semaphore_signal(
            barrier, inc=1, device_id={"gx": lax.rem(gx + k, n)}, device_id_type=MESH
        )
    for k in range(1, m):
        pl.semaphore_signal(
            barrier, inc=1, device_id={"gy": lax.rem(gy + k, m)}, device_id_type=MESH
        )

    def plane(i):
        return pl.ds(pl.multiple_of(i * ny, ny), ny)

    def row(j):
        return pl.ds(pl.multiple_of(j * nx, nx), nx)

    def across(j):
        return pl.ds(j, nx, stride=ny)

    def loop(count, body, init):
        return lax.fori_loop(0, count, body, init, unroll=8)

    lane = lax.broadcasted_iota(jnp.int32, (ny, nz), 1)
    sub = lax.broadcasted_iota(jnp.int32, (ny, nz), 0)
    zero_plane = jnp.zeros((ny, nz), jnp.float32)
    zero_row = jnp.zeros((nx, nz), jnp.float32)

    def f_z(v):
        return jnp.where(lane == nz - 1, 0.0, pltpu.roll(v, nz - 1, 1)) - v

    def b_z(v):
        return v - jnp.where(lane == 0, 0.0, pltpu.roll(v, 1, 1))

    def f_y(v, after):
        return jnp.where(sub == ny - 1, after, pltpu.roll(v, ny - 1, 0)) - v

    def b_y(v, before):
        return v - jnp.where(sub == 0, before, pltpu.roll(v, 1, 0))

    def near(src, dst, slot, device):
        return pltpu.make_async_remote_copy(
            src_ref=src, dst_ref=dst, send_sem=near_send.at[slot],
            recv_sem=near_recv.at[slot], device_id=device, device_id_type=MESH,
        )

    to_left = {"gx": jnp.maximum(gx - 1, 0)}
    to_right = {"gx": jnp.minimum(gx + 1, n - 1)}
    to_low = {"gy": jnp.maximum(gy - 1, 0)}
    to_high = {"gy": jnp.minimum(gy + 1, m - 1)}
    send_ey = near(fields.at[EY, pl.ds(0, ny)], ey_next, 0, to_left)
    send_hz = near(fields.at[HZ, pl.ds((nx - 1) * ny, ny)], hz_prev, 1, to_right)
    send_hx = near(hx_send, hx_prev, 2, to_high)
    send_ez = near(ez_send, ez_next, 3, to_low)
    send_v = near(rhs.at[pl.ds(0, ny)], v_next, 4, to_left)

    has_left = gx > 0
    has_right = gx < n - 1
    has_low = gy > 0
    has_high = gy < m - 1

    def start(cond, copy):
        @pl.when(cond)
        def _():
            copy.start()

    def sent(cond, copy):
        @pl.when(cond)
        def _():
            copy.wait_send()

    def arrived(cond, copy, ref):
        @pl.when(cond)
        def _():
            copy.wait_recv()

        @pl.when(jnp.logical_not(cond))
        def _():
            ref[...] = jnp.zeros(ref.shape, jnp.float32)


    def x_copy(kind, k, src, dst):
        target = lax.rem(gx + k, n)
        return pltpu.make_async_remote_copy(
            src_ref=src, dst_ref=dst.at[gx], send_sem=x_send.at[kind, k],
            recv_sem=x_recv.at[kind, gx], device_id={"gx": target}, device_id_type=MESH,
        )

    def y_copy(kind, k, src, dst):
        target = lax.rem(gy + k, m)
        return pltpu.make_async_remote_copy(
            src_ref=src, dst_ref=dst.at[gy], send_sem=y_send.at[kind, k],
            recv_sem=y_recv.at[kind, gy], device_id={"gy": target}, device_id_type=MESH,
        )

    def x_wait(kind, src, dst, j):
        pltpu.make_async_remote_copy(
            src_ref=src, dst_ref=dst.at[j], send_sem=x_send.at[kind, 0],
            recv_sem=x_recv.at[kind, j], device_id={"gx": j}, device_id_type=MESH,
        ).wait_recv()

    def y_wait(kind, src, dst, j):
        pltpu.make_async_remote_copy(
            src_ref=src, dst_ref=dst.at[j], send_sem=y_send.at[kind, 0],
            recv_sem=y_recv.at[kind, j], device_id={"gy": j}, device_id_type=MESH,
        ).wait_recv()

    def pick(label, lowest, width):
        if width == 1:
            return eps[lowest]
        half = width // 2
        return jnp.where(
            (label & half) != 0,
            pick(label, lowest + half, half),
            pick(label, lowest, half),
        )

    def coefficients(i, _):
        s = plane(i)
        label = region[s, :]
        eps_here = pick(label, 0, labels)
        small_k[s, :] = eps_here * (1.0 / 1024.0)
        ce[s, :] = 32.0 / eps_here
        return 0

    load_eps.wait()
    load_region.wait()
    loop(nx, coefficients, 0)
    pl.semaphore_wait(barrier, n + m - 2)
    loads[HX].wait()
    hx_send[...] = fields[HX, across(ny - 1), :]
    start(has_high, send_hx)
    loads[EY].wait()
    start(has_left, send_ey)
    loads[HZ].wait()
    start(has_right, send_hz)

    per = ny // nx

    def factor_step(small, carry, s, inv_ref, c_ref, l_ref):
        gap, d_last = carry
        total = small + gap
        c = 1.0 / (1.0 + total)
        d = c * d_last
        inv_ref[s, :] = c * small
        c_ref[s, :] = c
        l_ref[s, :] = d
        return total * c, d

    def factor_forward(i, carry):
        on_x, on_y = carry
        on_x = factor_step(small_k[plane(i), :], on_x, plane(i), inv_x, c_x, l_x)
        for k in range(per):
            j = i * per + k
            on_y = factor_step(small_k[across(j), :], on_y, row(j), inv_y, c_y, l_y)
        return on_x, on_y

    loop(nx, factor_forward, (
        (zero_plane + jnp.where(gx == 0, 0.0, 1.0), zero_plane + 1.0),
        (zero_row + jnp.where(gy == 0, 0.0, 1.0), zero_row + 1.0),
    ))

    def factor_back(carry, s, c_ref, l_ref, r_ref):
        l_after, r_after = carry
        c = c_ref[s, :]
        l = l_ref[s, :] + c * l_after
        r = c * r_after
        l_ref[s, :] = l
        r_ref[s, :] = r
        return l, r

    def factor_backward(t, carry):
        on_x, on_y = carry
        on_x = factor_back(on_x, plane(nx - 1 - t), c_x, l_x, r_x)
        for k in range(per):
            on_y = factor_back(on_y, row(ny - 1 - t * per - k), c_y, l_y, r_y)
        return on_x, on_y

    on_x, on_y = loop(
        nx, factor_backward, ((zero_plane, zero_plane + 1.0), (zero_row, zero_row + 1.0))
    )
    mx_send[0] = on_x[0]
    mx_send[1] = r_x[plane(nx - 1), :]
    mx_send[2] = on_x[1]
    for k in range(1, n):
        x_copy(0, k, mx_send, mx_recv).start()
    my_send[0] = on_y[0]
    my_send[1] = r_y[row(ny - 1), :]
    my_send[2] = on_y[1]
    for k in range(1, m):
        y_copy(0, k, my_send, my_recv).start()

    def backward_sweep(count, at, zero, c_ref, p_ref):
        def body(t, after):
            s = at(count - 1 - t)
            w = p_ref[s, :] + c_ref[s, :] * after
            p_ref[s, :] = w
            return w

        return loop(count, body, zero)

    def y_sweep():
        def body(j, last):
            s = row(j)
            d = rhs[across(j), :] * inv_y[s, :] + c_y[s, :] * last
            p_y[s, :] = d
            return d

        last = loop(ny, body, zero_row)
        return backward_sweep(ny, row, zero_row, c_y, p_y), last

    loads[EX].wait()
    loads[HY].wait()
    loads[EZ].wait()
    arrived(has_low, send_hx, hx_prev)

    def ez_forward(i, carry):
        q_last, d_last = carry
        s = plane(i)
        q = fields[HY, s, :] - 0.5 * f_z(fields[EX, s, :])
        coef = ce[s, :]
        r = fields[EZ, s, :] + coef * (
            (q - q_last) - b_y(fields[HX, s, :], hx_prev[pl.ds(i, 1), :])
        )
        d = r * inv_x[s, :] + c_x[s, :] * d_last
        p_x[s, :] = d
        return q, d

    q_end, ez_last = loop(nx, ez_forward, (zero_plane, zero_plane))
    sx_send[0, 0] = backward_sweep(nx, plane, zero_plane, c_x, p_x)
    sx_send[0, 1] = ez_last - q_end * 0.03125
    for k in range(1, n):
        x_copy(1, k, sx_send.at[0], sx_recv.at[0]).start()

    arrived(has_right, send_ey, ey_next)

    def ex_right(i, ey_after):
        i = nx - 1 - i
        s = plane(i)
        ey_here = fields[EY, s, :]
        p = fields[HZ, s, :] - 32.0 * (ey_after - ey_here)
        p1[s, :] = p
        coef = ce[s, :]
        rhs[s, :] = fields[EX, s, :] + coef * (
            b_y(p, 0.0) - 0.015625 * b_z(fields[HY, s, :])
        )
        return ey_here

    loop(nx, ex_right, ey_next[...])
    ex_first, ex_last = y_sweep()
    sy_send[0, 0] = ex_first
    sy_send[0, 1] = ex_last - p1[across(ny - 1), :] * 0.03125
    for k in range(1, m):
        y_copy(1, k, sy_send.at[0], sy_recv.at[0]).start()

    arrived(has_left, send_hz, hz_prev)

    def ey_one(i, hz_last):
        s = plane(i)
        hz_here = fields[HZ, s, :]
        ey1[s, :] = fields[EY, s, :] + ce[s, :] * (
            0.015625 * b_z(fields[HX, s, :]) - (hz_here - hz_last)
        )
        return hz_here

    loop(nx, ey_one, hz_prev[...])

    def reduce_matrix(me, count, wait, recv, own, one_ref, two_ref, coef, zero):
        def up(j, b):
            wait(j)
            rf = recv[j, 2]
            g = rf / (1.0 - b * recv[j, 0])
            one_ref[j] = g
            two_ref[j] = b
            return recv[j, 1] + g * b * rf

        b = lax.fori_loop(0, me, up, zero)

        def down(t, e):
            j = count - 1 - t
            wait(j)
            rf = recv[j, 2]
            h = rf / (1.0 - e * recv[j, 1])
            one_ref[j] = h
            two_ref[j] = e
            return recv[j, 0] + h * e * rf

        e = lax.fori_loop(0, count - 1 - me, down, zero)
        rf = own[2]
        one = 1.0 - b * own[0]
        two = 1.0 - e * own[1]
        scale = 1.0 / (one * two - (b * rf) * (e * rf))
        coef[0] = b
        coef[1] = e
        coef[2] = two * scale
        coef[3] = b * rf * scale
        coef[4] = e * rf * scale
        coef[5] = one * scale

    reduce_matrix(gx, n, lambda j: x_wait(0, mx_send, mx_recv, j),
                  mx_recv, mx_send, gx_one, gx_two, coef_x, zero_plane)
    reduce_matrix(gy, m, lambda j: y_wait(0, my_send, my_recv, j),
                  my_recv, my_send, gy_one, gy_two, coef_y, zero_row)

    def reduce_sides(me, count, wait, recv, own, one_ref, two_ref, coef, zero):
        def up(j, a):
            wait(j)
            return recv[j, 1] + one_ref[j] * (a + two_ref[j] * recv[j, 0])

        a = lax.fori_loop(0, me, up, zero)

        def down(t, c):
            j = count - 1 - t
            wait(j)
            return recv[j, 0] + one_ref[j] * (c + two_ref[j] * recv[j, 1])

        c = lax.fori_loop(0, count - 1 - me, down, zero)
        a = a + coef[0] * own[0]
        c = c + coef[1] * own[1]
        return coef[2] * a + coef[3] * c, coef[4] * a + coef[5] * c

    def x_sides(step):
        return reduce_sides(
            gx, n, lambda j: x_wait(1 + step, sx_send.at[step], sx_recv.at[step], j),
            sx_recv.at[step], sx_send.at[step], gx_one, gx_two, coef_x, zero_plane)

    def y_sides(step):
        return reduce_sides(
            gy, m, lambda j: y_wait(1 + step, sy_send.at[step], sy_recv.at[step], j),
            sy_recv.at[step], sy_send.at[step], gy_one, gy_two, coef_y, zero_row)

    wl, wr = x_sides(0)
    wr_x[...] = wr

    def ez_fill(i, _):
        s = plane(i)
        ez1[s, :] = p_x[s, :] + l_x[s, :] * wl + r_x[s, :] * wr
        return 0

    loop(nx, ez_fill, 0)
    ez_send[...] = ez1[across(0), :]
    start(has_low, send_ez)

    wl, wr = y_sides(0)
    wr_y[...] = wr

    def ex_fill(j, _):
        s = row(j)
        ex1[across(j), :] = p_y[s, :] + l_y[s, :] * wl + r_y[s, :] * wr
        return 0

    loop(ny, ex_fill, 0)

    def v_right(i, _):
        s = plane(i)
        g = f_z(ey1[s, :])
        rhs[s, :] = (
            3.0 * ez1[s, :] - fields[EZ, s, :] - ce[s, :] * b_y(g, 0.0)
        )
        out[HX, s, :] = fields[HX, s, :] + g
        return 0

    loop(nx, v_right, 0)
    arrived(has_high, send_ez, ez_next)

    def ey_forward(i, carry):
        p_last, d_last = carry
        s = plane(i)
        one = pl.ds(i, 1)
        p = p1[s, :] + 64.0 * f_y(ex1[s, :], wr_y[one, :])
        p2[s, :] = p
        ey = ey1[s, :]
        hx = fields[HX, s, :] - 32.0 * f_y(ez1[s, :], ez_next[one, :]) + 0.5 * f_z(ey)
        r = ey + ce[s, :] * (0.015625 * b_z(hx) - (p - p_last))
        d = r * inv_x[s, :] + c_x[s, :] * d_last
        p_x[s, :] = d
        return p, d

    p_end, ey_last = loop(nx, ey_forward, (zero_plane, zero_plane))
    sx_send[1, 0] = backward_sweep(nx, plane, zero_plane, c_x, p_x)
    sx_send[1, 1] = ey_last + p_end * 0.03125
    for k in range(1, n):
        x_copy(2, k, sx_send.at[1], sx_recv.at[1]).start()

    v_first, v_last = y_sweep()
    sy_send[1, 0] = v_first
    sy_send[1, 1] = v_last + 0.03125 * (
        out[HX, across(ny - 1), :] - fields[HX, across(ny - 1), :]
    )
    for k in range(1, m):
        y_copy(2, k, sy_send.at[1], sy_recv.at[1]).start()

    def ex_two(i, ez_after):
        i = nx - 1 - i
        s = plane(i)
        ex = fields[EX, s, :]
        ez_here = ez1[s, :]
        d_ex = 0.5 * f_z(ex)
        change = d_ex - 32.0 * (ez_after - ez_here)
        two = 2.0 * ex1[s, :] - ex + (0.015625 * ce[s, :]) * b_z(change)
        out[EX, s, :] = two
        out[HY, s, :] = fields[HY, s, :] - d_ex - 0.5 * f_z(two)
        return ez_here

    loop(nx, ex_two, wr_x[...])

    wl, wr = y_sides(1)
    wr_y[...] = wr

    def v_fill(j, _):
        s = row(j)
        rhs[across(j), :] = p_y[s, :] + l_y[s, :] * wl + r_y[s, :] * wr
        return 0

    loop(ny, v_fill, 0)
    start(has_left, send_v)

    def last_ez(i, _):
        s = plane(i)
        v = rhs[s, :]
        out[EZ, s, :] = v - ez1[s, :]
        out[HX, s, :] = out[HX, s, :] - 32.0 * f_y(v, wr_y[pl.ds(i, 1), :])
        return 0

    loop(nx, last_ez, 0)

    wl, wr = x_sides(1)

    def last_ey(t, after):
        s = plane(nx - 1 - t)
        w = p_x[s, :] + l_x[s, :] * wl + r_x[s, :] * wr
        out[EY, s, :] = w
        out[HZ, s, :] = p2[s, :] - 32.0 * (after - w)
        return w

    loop(nx, last_ey, wr)

    arrived(has_right, send_v, v_next)

    def last_hy(t, after):
        s = plane(nx - 1 - t)
        v = rhs[s, :]
        out[HY, s, :] = out[HY, s, :] + 32.0 * (after - v)
        return v

    loop(nx, last_hy, v_next[...])

    sent(has_left, send_ey)
    sent(has_right, send_hz)
    sent(has_high, send_hx)
    sent(has_low, send_ez)
    sent(has_left, send_v)
    for k in range(1, n):
        x_copy(0, k, mx_send, mx_recv).wait_send()
        x_copy(1, k, sx_send.at[0], sx_recv.at[0]).wait_send()
        x_copy(2, k, sx_send.at[1], sx_recv.at[1]).wait_send()
    for k in range(1, m):
        y_copy(0, k, my_send, my_recv).wait_send()
        y_copy(1, k, sy_send.at[0], sy_recv.at[0]).wait_send()
        y_copy(2, k, sy_send.at[1], sy_recv.at[1]).wait_send()


def local(n, m, fields, region, eps_table):
    _, nx, ny, nz = fields.shape
    cells = nx * ny
    labels = eps_table.shape[0]
    big = pltpu.VMEM((cells, nz), jnp.float32)
    x_row = pltpu.VMEM((ny, nz), jnp.float32)
    y_row = pltpu.VMEM((nx, nz), jnp.float32)

    def sided(width, count):
        return [
            pltpu.VMEM((3, width, nz), jnp.float32),
            pltpu.VMEM((count, 3, width, nz), jnp.float32),
            pltpu.VMEM((count, width, nz), jnp.float32),
            pltpu.VMEM((count, width, nz), jnp.float32),
            pltpu.VMEM((6, width, nz), jnp.float32),
            pltpu.VMEM((2, 2, width, nz), jnp.float32),
            pltpu.VMEM((2, count, 2, width, nz), jnp.float32),
        ]

    vmem = pl.BlockSpec(memory_space=pltpu.VMEM)
    result = pl.pallas_call(
        functools.partial(kernel, n, m, nx, ny, nz, labels),
        out_shape=pltpu.VMEM((6, cells, nz), jnp.float32),
        in_specs=[pl.BlockSpec(memory_space=pl.ANY)] * 3,
        out_specs=vmem,
        scratch_shapes=[
            pltpu.VMEM((6, cells, nz), jnp.float32),
            pltpu.VMEM((cells, nz), jnp.int32),
            pltpu.SMEM((labels,), jnp.float32),
        ]
        + [big] * 18
        + [x_row, x_row, y_row, y_row, y_row, y_row, x_row, x_row, y_row]
        + sided(ny, n)
        + sided(nx, m)
        + [
            pltpu.SemaphoreType.DMA((8,)),
            pltpu.SemaphoreType.DMA((5,)),
            pltpu.SemaphoreType.DMA((5,)),
            pltpu.SemaphoreType.DMA((3, n)),
            pltpu.SemaphoreType.DMA((3, n)),
            pltpu.SemaphoreType.DMA((3, m)),
            pltpu.SemaphoreType.DMA((3, m)),
        ],
        compiler_params=pltpu.CompilerParams(
            collective_id=0, has_side_effects=True, vmem_limit_bytes=60 * 1024 * 1024
        ),
    )(fields.reshape(6, cells, nz), region.reshape(cells, nz), eps_table)
    return result.reshape(fields.shape)


def solution(mesh):
    return jax.shard_map(
        functools.partial(local, mesh.shape["gx"], mesh.shape["gy"]),
        mesh=mesh,
        in_specs=(P(None, "gx", "gy", None), P("gx", "gy", None), P()),
        out_specs=P(None, "gx", "gy", None),
        check_vma=False,
    )
```
